32 devices in a mesh: ra: 8 (over z, x), dec: 4 (over y, core).
Axes of the slice: x: 2, y: 2, z: 4, core: 2. Of those that a mesh axis runs over, the one named last changes fastest.
Arguments:
- lens_block: bfloat16 [8, 4, 130, 512], P('ra', 'dec'), may hold values from 0 to 255, as said below
- lens_count: int32 [8, 4], P('ra', 'dec'), may hold values from 64 to 512, as said below
- lens_region: int32 [8, 4, 512], P('ra', 'dec'), may hold values from 0 to 255, as said below
- lens_sample: int32 [8, 4, 512], P('ra', 'dec'), may hold values from 0 to 7
- source_block: bfloat16 [8, 4, 133, 1024], P('ra', 'dec'), may hold values from -1 to 255, as said below
Outputs:
- jk_signal: float32 [256, 8, 20], P(('ra', 'dec'))
- jk_weight: float32 [256, 8, 20], P(('ra', 'dec'))
The draws below stay inside these ranges and needn't reach their ends.
Inputs may be any that keep to these rules, and one draw needn't show every extreme that they name: The live lenses of patch (i, j) fill its first lens_count[i, j] slots; each count is 512, 256, 128 or 64, and at least one patch is full. `lens_block`: the first 128 rows are zero or positive, and zero below the lens's own redshift bin; the last two rows are whole numbers from 0 to 255. `source_block`: the first 128 rows are zero or positive; positions are whole numbers from 0 to 255; weights are positive. `lens_region`: each id labels a compact area of the sky.
All inputs are finite; a program needn't handle non-finite values.
Results may differ from the reference program's by a relative error of at most 0.0003.
Values may be sent and summed in bfloat16 or wider, within the bound.
A program may use at most 64 MiB of HBM per device.

```python
import math
import jax
import jax.numpy as jnp
from jax import lax

ZBINS = 128
NBIN = 20
SAMPLES = 8
PATCH = 256
R_IN = 12
L_PATCH = 512
S_PATCH = 1024
REG_DEV = 8
COLUMNS = 8
BANDS = 4
REGIONS = 256


def lens_positions(key):
    key_x = jax.random.fold_in(key, 101)
    key_y = jax.random.fold_in(key, 102)
    position_x = jax.random.randint(key_x, (COLUMNS, BANDS, 1, L_PATCH), 0, PATCH)
    position_y = jax.random.randint(key_y, (COLUMNS, BANDS, 1, L_PATCH), 0, PATCH)
    return (position_x.astype(jnp.int32), position_y.astype(jnp.int32))


def draw_lens_count(key, part):
    key_levels, key_full = jax.random.split(key)
    halvings = jax.random.randint(key_levels, (COLUMNS, BANDS), 0, 4)
    chosen = jax.random.randint(key_full, (), 0, COLUMNS * BANDS)
    flat_index = jnp.arange(COLUMNS * BANDS).reshape(COLUMNS, BANDS)
    halvings = jnp.where(flat_index == chosen, 0, halvings)
    return (L_PATCH // jnp.left_shift(1, halvings)).astype(jnp.int32)


def draw_lens_region(key, part):
    position_x, position_y = lens_positions(key)
    margin = PATCH // 16
    column = jnp.arange(COLUMNS, dtype=jnp.int32).reshape(COLUMNS, 1, 1)
    band = jnp.arange(BANDS, dtype=jnp.int32).reshape(1, BANDS, 1)
    along = column * PATCH + position_x[:, :, 0, :] - margin
    along = jnp.mod(along, COLUMNS * PATCH)
    owner = along // PATCH
    stripe = along % PATCH * REG_DEV // PATCH
    spatial = (owner * BANDS + band) * REG_DEV + stripe
    labels = jax.random.permutation(jax.random.fold_in(key, 103), REGIONS).astype(jnp.int32)
    return jnp.take(labels, spatial).astype(jnp.int32)


def draw_lens_block(key, part):
    key_bins, key_factor = jax.random.split(key, 2)
    shape_kernel = (COLUMNS, BANDS, ZBINS, L_PATCH)
    lens_bin = jax.random.randint(key_bins, (COLUMNS, BANDS, 1, L_PATCH), 0, ZBINS // 2).astype(jnp.float32)
    levels = jnp.arange(ZBINS, dtype=jnp.float32).reshape(1, 1, ZBINS, 1)
    ramp_rows = jnp.maximum(levels - lens_bin, 0.0) / ZBINS
    factor = jnp.exp(jax.random.uniform(key_factor, shape_kernel, jnp.float32, -0.6931, 0.6931))
    kernel = 2.0 * ramp_rows * factor
    position_x, position_y = lens_positions(key)
    return jnp.concatenate([kernel, position_x.astype(jnp.float32), position_y.astype(jnp.float32)], axis=2).astype(jnp.bfloat16)


def bump(levels, middle, width):
    return jnp.exp(-0.5 * ((levels - middle) / width) ** 2) / (2.5066 * width)


def draw_source_block(key, part):
    key_list = jax.random.split(key, 12)
    shape_rows = (COLUMNS, BANDS, 1, S_PATCH)
    shape_pdf = (COLUMNS, BANDS, ZBINS, S_PATCH)
    center = jax.random.uniform(key_list[0], shape_rows, jnp.float32, 8.0, ZBINS - 8.0)
    spread = jax.random.uniform(key_list[1], shape_rows, jnp.float32, 2.0, 8.0)
    center_two = jax.random.uniform(key_list[8], shape_rows, jnp.float32, 4.0, ZBINS - 4.0)
    spread_two = jax.random.uniform(key_list[9], shape_rows, jnp.float32, 3.0, 10.0)
    center_wide = jax.random.uniform(key_list[10], shape_rows, jnp.float32, 0.25 * ZBINS, 0.75 * ZBINS)
    spread_wide = jax.random.uniform(key_list[11], shape_rows, jnp.float32, 20.0, 40.0)
    levels = jnp.arange(ZBINS, dtype=jnp.float32).reshape(1, 1, ZBINS, 1)
    rough_factor = jnp.exp(jax.random.uniform(key_list[2], shape_pdf, jnp.float32, -0.6931, 0.6931))
    shear_one = 0.25 * jax.random.truncated_normal(key_list[3], -3.6, 3.6, shape_rows, jnp.float32)
    shear_two = 0.25 * jax.random.truncated_normal(key_list[4], -3.6, 3.6, shape_rows, jnp.float32)
    weight = jnp.exp(jax.random.uniform(key_list[5], shape_rows, jnp.float32, math.log(0.3), math.log(3.0)))
    profile = 0.6 * bump(levels, center, spread) + 0.25 * bump(levels, center_two, spread_two)
    profile = profile + 0.1 * bump(levels, center_wide, spread_wide) + 0.05 / ZBINS
    pdf_rows = profile * rough_factor
    position_x = jax.random.randint(key_list[6], shape_rows, 0, PATCH).astype(jnp.float32)
    position_y = jax.random.randint(key_list[7], shape_rows, 0, PATCH).astype(jnp.float32)
    return jnp.concatenate([pdf_rows, position_x, position_y, shear_one, shear_two, weight], axis=2).astype(jnp.bfloat16)


def place_ends(values, own_key, low, top_value):
    longest = values.shape.index(max(values.shape))
    spots = []
    for shift in (0, 1):
        where = [jax.random.randint(jax.random.fold_in(own_key, axis), (), 0, length) for axis, length in enumerate(values.shape)]
        where[longest] = (where[longest] + shift) % values.shape[longest]
        spots.append(tuple(where))
    return values.at[spots[0]].set(low).at[spots[1]].set(top_value)


def setup_inputs(seed: int = 0) -> dict:
    arg_keys = jax.random.split(jax.random.key(seed), 6)
    lens_block = draw_lens_block(jax.random.fold_in(arg_keys[5], 71), 0)
    lens_count = draw_lens_count(jax.random.fold_in(arg_keys[5], 71), 0)
    lens_region = draw_lens_region(jax.random.fold_in(arg_keys[5], 71), 0)
    lens_sample = place_ends(jax.random.randint(arg_keys[3], (COLUMNS, BANDS, L_PATCH), 0, SAMPLES), jax.random.fold_in(arg_keys[3], 1), 0, SAMPLES - 1).astype(jnp.int32)
    source_block = draw_source_block(jax.random.fold_in(arg_keys[5], 71), 0)
    return {"lens_block": lens_block, "lens_count": lens_count, "lens_region": lens_region, "lens_sample": lens_sample, "source_block": source_block}


growth_top = 23
growth_bottom = 20

def edge_squares():
    return [float((R_IN * growth_top ** edge_level // growth_bottom ** edge_level) ** 2) for edge_level in range(NBIN + 1)]

def bin_scales():
    edge_sq = edge_squares()
    lens_per_cell = L_PATCH / (SAMPLES * REG_DEV)
    density = S_PATCH / (PATCH * PATCH)
    expected = [math.pi * (edge_sq[edge_level + 1] - edge_sq[edge_level]) * density * lens_per_cell for edge_level in range(NBIN)]
    return jnp.array(expected, jnp.float32)

def pair_sums(kernel_tile, lens_x, lens_y, source_rows, edge_sq):
    pdf_bins = kernel_tile.shape[0]
    inverse_crit = lax.dot_general(kernel_tile, source_rows[:pdf_bins], (((0,), (0,)), ((), ())), preferred_element_type=jnp.float32)
    catalog = source_rows[pdf_bins:].astype(jnp.float32)
    delta_x = catalog[0][None, :] - lens_x[:, None]
    delta_y = catalog[1][None, :] - lens_y[:, None]
    radius_sq = delta_x * delta_x + delta_y * delta_y
    safe_sq = jnp.maximum(radius_sq, edge_sq[0])
    cos_two = (delta_x * delta_x - delta_y * delta_y) / safe_sq
    sin_two = 2.0 * delta_x * delta_y / safe_sq
    tangent = -(catalog[2][None, :] * cos_two + catalog[3][None, :] * sin_two)
    weighted = catalog[4][None, :] * inverse_crit
    signal = weighted * tangent
    weight = weighted * inverse_crit
    lower_sq = jnp.array(edge_sq[:-1], jnp.float32)[:, None, None]
    upper_sq = jnp.array(edge_sq[1:], jnp.float32)[:, None, None]
    inside = (radius_sq[None] >= lower_sq) & (radius_sq[None] < upper_sq)
    signal_bins = lax.optimization_barrier(jnp.sum(jnp.where(inside, signal[None], 0.0), axis=2))
    weight_bins = lax.optimization_barrier(jnp.sum(jnp.where(inside, weight[None], 0.0), axis=2))
    return jnp.stack([signal_bins, weight_bins], axis=0)

def local_terms(lens_tile, neighbours, edge_sq):
    pdf_bins = lens_tile.shape[0] - 2
    kernel_tile = lens_tile[:pdf_bins]
    lens_x = lens_tile[pdf_bins].astype(jnp.float32)
    lens_y = lens_tile[pdf_bins + 1].astype(jnp.float32)
    totals = jnp.zeros((2, len(edge_sq) - 1, lens_tile.shape[1]), jnp.float32)
    for shift_x in (-1, 0, 1):
        for shift_y in (-1, 0, 1):
            source_rows = neighbours[3 * (shift_x + 1) + shift_y + 1]
            totals = totals + pair_sums(kernel_tile, lens_x - shift_x * PATCH, lens_y - shift_y * PATCH, source_rows, edge_sq)
    return totals

def reference(lens_block, lens_count, lens_region, lens_sample, source_block):
    edge_sq = edge_squares()
    padded = jnp.pad(source_block, ((0, 0), (1, 1), (0, 0), (0, 0)))
    tile_rows = math.gcd(L_PATCH, 128)
    starts = jnp.arange(L_PATCH // tile_rows, dtype=jnp.int32) * tile_rows

    def patch_terms(patch_index):
        column = patch_index // BANDS
        row_index = patch_index % BANDS
        lenses = lens_block[column, row_index]
        neighbours = []
        for shift_x in (-1, 0, 1):
            for shift_y in (-1, 0, 1):
                neighbours.append(padded[(column + shift_x) % COLUMNS, row_index + 1 + shift_y])

        def tile_terms(first_lens):
            lens_tile = lax.dynamic_slice_in_dim(lenses, first_lens, tile_rows, 1)
            return local_terms(lens_tile, neighbours, edge_sq)
        pieces = lax.map(tile_terms, starts)
        totals = jnp.transpose(pieces, (1, 2, 0, 3)).reshape(2, NBIN, L_PATCH)
        live_lens = jnp.arange(L_PATCH, dtype=jnp.int32) < lens_count[column, row_index]
        return jnp.where(live_lens[None, None, :], totals, 0.0)
    per_patch = lax.map(patch_terms, jnp.arange(COLUMNS * BANDS, dtype=jnp.int32))
    per_lens = jnp.transpose(per_patch, (0, 3, 1, 2)).reshape(COLUMNS * BANDS * L_PATCH, 2 * NBIN)
    segment = (lens_region * SAMPLES + lens_sample).reshape(-1).astype(jnp.int32)
    region_table = jax.ops.segment_sum(per_lens, segment, num_segments=REGIONS * SAMPLES)
    region_table = region_table.reshape(REGIONS, SAMPLES, 2, NBIN)
    scales = bin_scales()
    return (region_table[:, :, 0, :] / jnp.sqrt(scales), region_table[:, :, 1, :] / scales)
```

```python
import functools
import math

import jax
import jax.numpy as jnp
from jax import lax
from jax.experimental import pallas as pl
from jax.experimental.pallas import tpu as pltpu
from jax.sharding import PartitionSpec as P

NBIN = 20
SAMPLES = 8
PATCH = 256
R_IN = 12
L_PATCH = 512
S_PATCH = 1024
REG_DEV = 8


growth_top = 23
growth_bottom = 20


def extended(block, sides, width, periodic):
    for axis, dim in sides:
        count = lax.axis_size(axis)
        forward = [(i, i + 1) for i in range(count - 1)]
        if periodic:
            forward.append((count - 1, 0))
        backward = [(target, source) for source, target in forward]
        low = lax.ppermute(
            lax.slice_in_dim(block, block.shape[dim] - width, None, axis=dim), axis, forward
        )
        high = lax.ppermute(lax.slice_in_dim(block, 0, width, axis=dim), axis, backward)
        block = jnp.concatenate([low, block, high], axis=dim)
    return block


def edge_squares():
    return [
        float((R_IN * growth_top**edge_level // growth_bottom**edge_level) ** 2)
        for edge_level in range(NBIN + 1)
    ]


def bin_scales():
    edge_sq = edge_squares()
    lens_per_cell = L_PATCH / (SAMPLES * REG_DEV)
    density = S_PATCH / (PATCH * PATCH)
    expected = [
        math.pi * (edge_sq[edge_level + 1] - edge_sq[edge_level]) * density * lens_per_cell
        for edge_level in range(NBIN)
    ]
    return jnp.array(expected, jnp.float32)


def ranks(keys):
    total = keys.shape[0]
    unique = keys * total + jnp.arange(total, dtype=jnp.int32)
    return jnp.sum((unique[None, :] < unique[:, None]).astype(jnp.int32), axis=1)


def compact_order(position_x, position_y, dead, strip_size):
    strip = ranks(position_x + 2 * PATCH * dead) // strip_size
    return ranks(strip * (4 * PATCH) + position_y + 2 * PATCH * dead)


def pair_kernel(edge_sq, groups, chunk, class_ref, lens_ref, x_ref, y_ref, source_ref, catalog_ref, out_ref, crit, sums):
    patches, _, width = source_ref.shape
    tile = out_ref.shape[2]
    tiles = out_ref.shape[0]
    pieces = width // chunk

    def crit_step(patch, carry):
        crit[patch] = jnp.dot(lens_ref[...], source_ref[patch], preferred_element_type=jnp.float32)
        return carry

    lax.fori_loop(0, patches, crit_step, 0)

    def visit(first_edge, tile_index, patch, piece):
        rows = pl.ds(pl.multiple_of(tile_index * tile, tile), tile)
        lens_x = x_ref[rows, :]
        lens_y = y_ref[rows, :]
        parts = []
        for part in range(chunk // 128):
            columns = pl.ds(pl.multiple_of(piece * chunk + part * 128, 128), 128)
            inverse_crit = crit[patch, rows, columns]
            catalog = catalog_ref[patch, :, columns]
            delta_x = catalog[0:1] - lens_x
            delta_y = catalog[1:2] - lens_y
            square_x = delta_x * delta_x
            square_y = delta_y * delta_y
            radius_sq = square_x + square_y
            inverse = 1.0 / jnp.maximum(radius_sq, edge_sq[0])
            turned = catalog[2:3] * (square_x - square_y) + catalog[3:4] * (delta_x * delta_y)
            signal = inverse_crit * (turned * inverse)
            weight = catalog[4:5] * inverse_crit * inverse_crit
            parts.append((radius_sq, signal, weight))
        for edge in range(first_edge, len(edge_sq)):
            masks = [radius_sq < edge_sq[edge] for radius_sq, _, _ in parts]
            signal_sum = sum(jnp.where(m, part[1], 0.0) for m, part in zip(masks, parts))
            weight_sum = sum(jnp.where(m, part[2], 0.0) for m, part in zip(masks, parts))
            sums[edge, 0] += signal_sum
            sums[edge, 1] += weight_sum

    def tile_step(tile_index, carry):
        sums[...] = jnp.zeros_like(sums)

        def chunk_step(index, inner):
            chosen = class_ref[tile_index, index]
            for number, first_edge in enumerate(groups):
                @pl.when(chosen == number)
                def _():
                    visit(first_edge, tile_index, index // pieces, index % pieces)
            return inner

        lax.fori_loop(0, patches * pieces, chunk_step, 0)
        totals = jnp.sum(sums[...], axis=3)
        out_ref[tile_index] = jnp.concatenate(
            [totals[1:, 0] - totals[:-1, 0], totals[1:, 1] - totals[:-1, 1]], axis=0
        )
        return carry

    def guarded_step(tile_index, carry):
        @pl.when(class_ref[tile_index, patches * pieces] > 0)
        def _():
            tile_step(tile_index, 0)

        @pl.when(class_ref[tile_index, patches * pieces] <= 0)
        def _():
            out_ref[tile_index] = jnp.zeros(out_ref.shape[1:], jnp.float32)

        return carry

    lax.fori_loop(0, tiles, guarded_step, 0)


def on_device(lens_block, lens_count, lens_region, lens_sample, source_block):
    edge_sq = edge_squares()
    pdf_bins = source_block.shape[2] - 5
    width = source_block.shape[3]
    lens_total = lens_block.shape[3]
    tile = 32
    chunk = 256
    pieces = width // chunk
    groups = (0, 13, 17, 20)
    live_count = lens_count[0, 0]

    sources = source_block[0, 0]
    source_x = sources[pdf_bins].astype(jnp.int32)
    source_y = sources[pdf_bins + 1].astype(jnp.int32)
    source_rank = compact_order(source_x, source_y, jnp.zeros_like(source_x), width // 2)
    picked = (source_rank[:, None] == jnp.arange(width, dtype=jnp.int32)[None, :]).astype(jnp.bfloat16)
    sources = jnp.dot(sources, picked, preferred_element_type=jnp.float32).astype(jnp.bfloat16)
    partial_rows = extended(sources[None, None], (("ra", 0),), 1, True)
    beside_all = extended(partial_rows, (("dec", 1),), 1, False)
    beside_all = beside_all.reshape(9, sources.shape[0], width)

    lenses = lens_block[0, 0]
    slots = jnp.arange(lens_total, dtype=jnp.int32)
    dead = (slots >= live_count).astype(jnp.int32)
    lens_rank = compact_order(
        lenses[pdf_bins].astype(jnp.int32), lenses[pdf_bins + 1].astype(jnp.int32), dead, lens_total // 4
    )
    lens_hit = lens_rank[None, :] == slots[:, None]
    sorted_lenses = lax.dot_general(
        lens_hit.astype(jnp.bfloat16), lenses, (((1,), (1,)), ((), ())), preferred_element_type=jnp.float32
    )
    segment = lens_region[0, 0] * SAMPLES + lens_sample[0, 0]
    segment = jnp.sum(jnp.where(lens_hit, segment[None, :], 0), axis=1)
    lens_kernel = sorted_lenses[:, :pdf_bins].astype(jnp.bfloat16)
    lens_x = sorted_lenses[:, pdf_bins]
    lens_y = sorted_lenses[:, pdf_bins + 1]

    catalog = beside_all[:, pdf_bins:].astype(jnp.float32)
    shift = jnp.arange(9, dtype=jnp.int32)
    shift_x = ((shift // 3 - 1) * PATCH).astype(jnp.float32)[:, None]
    shift_y = ((shift % 3 - 1) * PATCH).astype(jnp.float32)[:, None]
    placed_x = catalog[:, 0] + shift_x
    placed_y = catalog[:, 1] + shift_y
    source_weight = catalog[:, 4]
    zero_row = jnp.zeros_like(placed_x)
    rows = jnp.stack(
        [
            placed_x,
            placed_y,
            -source_weight * catalog[:, 2],
            -2.0 * source_weight * catalog[:, 3],
            source_weight,
            zero_row,
            zero_row,
            zero_row,
        ],
        axis=1,
    )

    def gap(lens_at, source_at):
        lens_at = lens_at.reshape(-1, 1, tile)
        source_at = source_at.reshape(1, -1, chunk)
        apart = jnp.maximum(
            source_at.min(axis=2) - lens_at.max(axis=2), lens_at.min(axis=2) - source_at.max(axis=2)
        )
        return jnp.maximum(apart, 0.0)

    gap_x = gap(lens_x, placed_x)
    gap_y = gap(lens_y, placed_y)
    nearest_sq = gap_x * gap_x + gap_y * gap_y
    classes = sum((nearest_sq >= edge_sq[first - 1]).astype(jnp.int32) for first in groups[1:])
    classes = classes + (nearest_sq >= edge_sq[-1]).astype(jnp.int32)
    live_tile = (jnp.arange(lens_total // tile, dtype=jnp.int32) * tile < live_count).astype(jnp.int32)
    classes = jnp.concatenate([classes, live_tile[:, None]], axis=1)

    totals = pl.pallas_call(
        functools.partial(pair_kernel, edge_sq, groups, chunk),
        out_shape=jax.ShapeDtypeStruct((lens_total // tile, 2 * NBIN, tile), jnp.float32),
        in_specs=[pl.BlockSpec(memory_space=pltpu.SMEM)] + [pl.BlockSpec(memory_space=pltpu.VMEM)] * 5,
        out_specs=pl.BlockSpec(memory_space=pltpu.VMEM),
        scratch_shapes=[
            pltpu.VMEM((9, lens_total, width), jnp.float32),
            pltpu.VMEM((NBIN + 1, 2, tile, 128), jnp.float32),
        ],
        compiler_params=pltpu.CompilerParams(vmem_limit_bytes=48 * 2**20),
    )(
        classes,
        lens_kernel,
        jnp.broadcast_to(lens_x[:, None], (lens_total, 128)),
        jnp.broadcast_to(lens_y[:, None], (lens_total, 128)),
        beside_all[:, :pdf_bins],
        rows,
    )
    per_lens = jnp.transpose(totals, (0, 2, 1)).reshape(lens_total, 2 * NBIN)
    per_lens = jnp.where((slots < live_count)[:, None], per_lens, 0.0)
    devices = lax.axis_size("ra") * lax.axis_size("dec")
    region_table = jax.ops.segment_sum(per_lens, segment, num_segments=REG_DEV * devices * SAMPLES)
    region_table = region_table.reshape(devices, REG_DEV * SAMPLES * 2 * NBIN)
    received = lax.all_to_all(region_table, ("ra", "dec"), 0, 0, tiled=True)
    owned_rows = jnp.sum(received, axis=0).reshape(-1, SAMPLES, 2, NBIN)
    scales = bin_scales()
    return (owned_rows[:, :, 0, :] / jnp.sqrt(scales), owned_rows[:, :, 1, :] / scales)


def solution(mesh):
    placed = (
        P("ra", "dec", None, None),
        P("ra", "dec"),
        P("ra", "dec", None),
        P("ra", "dec", None),
        P("ra", "dec", None, None),
    )
    return jax.shard_map(
        on_device,
        mesh=mesh,
        in_specs=placed,
        out_specs=(P(("ra", "dec"), None, None), P(("ra", "dec"), None, None)),
        check_vma=False,
    )
```

```python
import functools
import math

import jax
import jax.numpy as jnp
from jax import lax
from jax.experimental import pallas as pl
from jax.experimental.pallas import tpu as pltpu
from jax.sharding import PartitionSpec as P

NBIN = 20
SAMPLES = 8
PATCH = 256
R_IN = 12
L_PATCH = 512
S_PATCH = 1024
REG_DEV = 8


growth_top = 23
growth_bottom = 20


def extended(block, sides, width, periodic):
    for axis, dim in sides:
        count = lax.axis_size(axis)
        forward = [(i, i + 1) for i in range(count - 1)]
        if periodic:
            forward.append((count - 1, 0))
        backward = [(target, source) for source, target in forward]
        low = lax.ppermute(
            lax.slice_in_dim(block, block.shape[dim] - width, None, axis=dim), axis, forward
        )
        high = lax.ppermute(lax.slice_in_dim(block, 0, width, axis=dim), axis, backward)
        block = jnp.concatenate([low, block, high], axis=dim)
    return block


def edge_squares():
    return [
        float((R_IN * growth_top**edge_level // growth_bottom**edge_level) ** 2)
        for edge_level in range(NBIN + 1)
    ]


def bin_scales():
    edge_sq = edge_squares()
    lens_per_cell = L_PATCH / (SAMPLES * REG_DEV)
    density = S_PATCH / (PATCH * PATCH)
    expected = [
        math.pi * (edge_sq[edge_level + 1] - edge_sq[edge_level]) * density * lens_per_cell
        for edge_level in range(NBIN)
    ]
    return jnp.array(expected, jnp.float32)


def ranks(keys):
    total = keys.shape[0]
    unique = keys * total + jnp.arange(total, dtype=jnp.int32)
    return jnp.sum((unique[None, :] < unique[:, None]).astype(jnp.int32), axis=1)


def compact_order(position_x, position_y, dead, strip_size):
    strip = ranks(position_x + 2 * PATCH * dead) // strip_size
    return ranks(strip * (4 * PATCH) + position_y + 2 * PATCH * dead)


def pair_kernel(edge_sq, groups, chunk, class_ref, lens_ref, x_ref, y_ref, source_ref, catalog_ref, out_ref, crit, sums):
    patches, _, width = source_ref.shape
    tile = out_ref.shape[2]
    tiles = out_ref.shape[0]
    pieces = width // chunk

    def crit_step(patch, carry):
        crit[patch] = jnp.dot(lens_ref[...], source_ref[patch], preferred_element_type=jnp.float32)
        return carry

    lax.fori_loop(0, patches, crit_step, 0)

    def visit(first_edge, tile_index, patch, piece):
        rows = pl.ds(pl.multiple_of(tile_index * tile, tile), tile)
        lens_x = x_ref[rows, :]
        lens_y = y_ref[rows, :]
        parts = []
        for part in range(chunk // 128):
            columns = pl.ds(pl.multiple_of(piece * chunk + part * 128, 128), 128)
            inverse_crit = crit[patch, rows, columns]
            catalog = catalog_ref[patch, :, columns]
            delta_x = catalog[0:1] - lens_x
            delta_y = catalog[1:2] - lens_y
            square_x = delta_x * delta_x
            square_y = delta_y * delta_y
            radius_sq = square_x + square_y
            inverse = 1.0 / jnp.maximum(radius_sq, edge_sq[0])
            turned = catalog[2:3] * (square_x - square_y) + catalog[3:4] * (delta_x * delta_y)
            signal = inverse_crit * (turned * inverse)
            weight = catalog[4:5] * inverse_crit * inverse_crit
            parts.append((radius_sq, signal, weight))
        for edge in range(first_edge, len(edge_sq)):
            masks = [radius_sq < edge_sq[edge] for radius_sq, _, _ in parts]
            signal_sum = sum(jnp.where(m, part[1], 0.0) for m, part in zip(masks, parts))
            weight_sum = sum(jnp.where(m, part[2], 0.0) for m, part in zip(masks, parts))
            sums[edge, 0] += signal_sum
            sums[edge, 1] += weight_sum

    def tile_step(tile_index, carry):
        sums[...] = jnp.zeros_like(sums)

        def chunk_step(index, inner):
            chosen = class_ref[tile_index, index]
            for number, first_edge in enumerate(groups):
                @pl.when(chosen == number)
                def _():
                    visit(first_edge, tile_index, index // pieces, index % pieces)
            return inner

        lax.fori_loop(0, patches * pieces, chunk_step, 0)
        totals = jnp.sum(sums[...], axis=3)
        out_ref[tile_index] = jnp.concatenate(
            [totals[1:, 0] - totals[:-1, 0], totals[1:, 1] - totals[:-1, 1]], axis=0
        )
        return carry

    def guarded_step(tile_index, carry):
        @pl.when(class_ref[tile_index, patches * pieces] > 0)
        def _():
            tile_step(tile_index, 0)

        @pl.when(class_ref[tile_index, patches * pieces] <= 0)
        def _():
            out_ref[tile_index] = jnp.zeros(out_ref.shape[1:], jnp.float32)

        return carry

    lax.fori_loop(0, tiles, guarded_step, 0)


def exchange_sum_kernel(table_ref, out_ref, first, partial, second, send_one, recv_one, send_two, recv_two):
    me_ra, me_dec = lax.axis_index("ra"), lax.axis_index("dec")
    count_ra, count_dec = lax.axis_size("ra"), lax.axis_size("dec")

    def peer_ra(step):
        return (lax.rem(me_ra + step, count_ra), me_dec)

    def peer_dec(step):
        return (me_ra, lax.rem(me_dec + step, count_dec))

    mesh_ids = pl.DeviceIdType.MESH
    barrier = pltpu.get_barrier_semaphore()
    for step in range(1, count_dec):
        pl.semaphore_signal(barrier, inc=1, device_id=peer_dec(step), device_id_type=mesh_ids)
    for step in range(1, count_ra):
        pl.semaphore_signal(barrier, inc=1, device_id=peer_ra(step), device_id_type=mesh_ids)
    pl.semaphore_wait(barrier, count_dec + count_ra - 2)

    copies = []
    for step in range(1, count_dec):
        copy = pltpu.make_async_remote_copy(
            src_ref=table_ref.at[lax.rem(me_dec + step, count_dec)],
            dst_ref=first.at[step - 1],
            send_sem=send_one.at[step - 1],
            recv_sem=recv_one.at[step - 1],
            device_id=peer_dec(step),
            device_id_type=mesh_ids,
        )
        copy.start()
        copies.append(copy)
    partial[...] = table_ref[me_dec]
    for step in range(1, count_dec):
        copies[step - 1].wait_recv()
        partial[...] += first[step - 1]
    late = []
    for step in range(1, count_ra):
        copy = pltpu.make_async_remote_copy(
            src_ref=partial.at[lax.rem(me_ra + step, count_ra)],
            dst_ref=second.at[step - 1],
            send_sem=send_two.at[step - 1],
            recv_sem=recv_two.at[step - 1],
            device_id=peer_ra(step),
            device_id_type=mesh_ids,
        )
        copy.start()
        late.append(copy)
    total = partial[me_ra]
    for step in range(1, count_ra):
        late[step - 1].wait_recv()
        total = total + second[step - 1]
    out_ref[...] = total
    for copy in copies + late:
        copy.wait_send()


def exchange_sum(table):
    count_dec, count_ra, rows, columns = table.shape
    return pl.pallas_call(
        exchange_sum_kernel,
        out_shape=jax.ShapeDtypeStruct((rows, columns), jnp.float32),
        in_specs=[pl.BlockSpec(memory_space=pltpu.VMEM)],
        out_specs=pl.BlockSpec(memory_space=pltpu.VMEM),
        scratch_shapes=[
            pltpu.VMEM((count_dec - 1, count_ra, rows, columns), jnp.float32),
            pltpu.VMEM((count_ra, rows, columns), jnp.float32),
            pltpu.VMEM((count_ra - 1, rows, columns), jnp.float32),
            pltpu.SemaphoreType.DMA((count_dec - 1,)),
            pltpu.SemaphoreType.DMA((count_dec - 1,)),
            pltpu.SemaphoreType.DMA((count_ra - 1,)),
            pltpu.SemaphoreType.DMA((count_ra - 1,)),
        ],
        compiler_params=pltpu.CompilerParams(
            collective_id=0, has_side_effects=True, vmem_limit_bytes=32 * 2**20
        ),
    )(table)


def on_device(lens_block, lens_count, lens_region, lens_sample, source_block):
    edge_sq = edge_squares()
    pdf_bins = source_block.shape[2] - 5
    width = source_block.shape[3]
    lens_total = lens_block.shape[3]
    tile = 32
    chunk = 256
    pieces = width // chunk
    groups = (0, 13, 17, 20)
    live_count = lens_count[0, 0]

    sources = source_block[0, 0]
    source_x = sources[pdf_bins].astype(jnp.int32)
    source_y = sources[pdf_bins + 1].astype(jnp.int32)
    source_rank = compact_order(source_x, source_y, jnp.zeros_like(source_x), width // 2)
    picked = (source_rank[:, None] == jnp.arange(width, dtype=jnp.int32)[None, :]).astype(jnp.bfloat16)
    sources = jnp.dot(sources, picked, preferred_element_type=jnp.float32).astype(jnp.bfloat16)
    partial_rows = extended(sources[None, None], (("ra", 0),), 1, True)
    beside_all = extended(partial_rows, (("dec", 1),), 1, False)
    beside_all = beside_all.reshape(9, sources.shape[0], width)

    lenses = lens_block[0, 0]
    slots = jnp.arange(lens_total, dtype=jnp.int32)
    dead = (slots >= live_count).astype(jnp.int32)
    lens_rank = compact_order(
        lenses[pdf_bins].astype(jnp.int32), lenses[pdf_bins + 1].astype(jnp.int32), dead, lens_total // 4
    )
    lens_hit = lens_rank[None, :] == slots[:, None]
    sorted_lenses = lax.dot_general(
        lens_hit.astype(jnp.bfloat16), lenses, (((1,), (1,)), ((), ())), preferred_element_type=jnp.float32
    )
    owner = lens_region[0, 0] // REG_DEV
    count_dec = lax.axis_size("dec")
    owner = owner % count_dec * lax.axis_size("ra") + owner // count_dec
    segment = (owner * REG_DEV + lens_region[0, 0] % REG_DEV) * SAMPLES + lens_sample[0, 0]
    segment = jnp.sum(jnp.where(lens_hit, segment[None, :], 0), axis=1)
    lens_kernel = sorted_lenses[:, :pdf_bins].astype(jnp.bfloat16)
    lens_x = sorted_lenses[:, pdf_bins]
    lens_y = sorted_lenses[:, pdf_bins + 1]

    catalog = beside_all[:, pdf_bins:].astype(jnp.float32)
    shift = jnp.arange(9, dtype=jnp.int32)
    shift_x = ((shift // 3 - 1) * PATCH).astype(jnp.float32)[:, None]
    shift_y = ((shift % 3 - 1) * PATCH).astype(jnp.float32)[:, None]
    placed_x = catalog[:, 0] + shift_x
    placed_y = catalog[:, 1] + shift_y
    source_weight = catalog[:, 4]
    zero_row = jnp.zeros_like(placed_x)
    rows = jnp.stack(
        [
            placed_x,
            placed_y,
            -source_weight * catalog[:, 2],
            -2.0 * source_weight * catalog[:, 3],
            source_weight,
            zero_row,
            zero_row,
            zero_row,
        ],
        axis=1,
    )

    def gap(lens_at, source_at):
        lens_at = lens_at.reshape(-1, 1, tile)
        source_at = source_at.reshape(1, -1, chunk)
        apart = jnp.maximum(
            source_at.min(axis=2) - lens_at.max(axis=2), lens_at.min(axis=2) - source_at.max(axis=2)
        )
        return jnp.maximum(apart, 0.0)

    gap_x = gap(lens_x, placed_x)
    gap_y = gap(lens_y, placed_y)
    nearest_sq = gap_x * gap_x + gap_y * gap_y
    classes = sum((nearest_sq >= edge_sq[first - 1]).astype(jnp.int32) for first in groups[1:])
    classes = classes + (nearest_sq >= edge_sq[-1]).astype(jnp.int32)
    live_tile = (jnp.arange(lens_total // tile, dtype=jnp.int32) * tile < live_count).astype(jnp.int32)
    classes = jnp.concatenate([classes, live_tile[:, None]], axis=1)

    totals = pl.pallas_call(
        functools.partial(pair_kernel, edge_sq, groups, chunk),
        out_shape=jax.ShapeDtypeStruct((lens_total // tile, 2 * NBIN, tile), jnp.float32),
        in_specs=[pl.BlockSpec(memory_space=pltpu.SMEM)] + [pl.BlockSpec(memory_space=pltpu.VMEM)] * 5,
        out_specs=pl.BlockSpec(memory_space=pltpu.VMEM),
        scratch_shapes=[
            pltpu.VMEM((9, lens_total, width), jnp.float32),
            pltpu.VMEM((NBIN + 1, 2, tile, 128), jnp.float32),
        ],
        compiler_params=pltpu.CompilerParams(vmem_limit_bytes=48 * 2**20),
    )(
        classes,
        lens_kernel,
        jnp.broadcast_to(lens_x[:, None], (lens_total, 128)),
        jnp.broadcast_to(lens_y[:, None], (lens_total, 128)),
        beside_all[:, :pdf_bins],
        rows,
    )
    per_lens = jnp.transpose(totals, (0, 2, 1)).reshape(lens_total, 2 * NBIN)
    per_lens = jnp.where((slots < live_count)[:, None], per_lens, 0.0)
    count_ra, count_dec = lax.axis_size("ra"), lax.axis_size("dec")
    region_table = jax.ops.segment_sum(per_lens, segment, num_segments=REG_DEV * count_ra * count_dec * SAMPLES)
    region_table = region_table.reshape(count_dec, count_ra, REG_DEV * SAMPLES * 2 * NBIN // 128, 128)
    owned_rows = exchange_sum(region_table).reshape(-1, SAMPLES, 2, NBIN)
    scales = bin_scales()
    return (owned_rows[:, :, 0, :] / jnp.sqrt(scales), owned_rows[:, :, 1, :] / scales)


def solution(mesh):
    placed = (
        P("ra", "dec", None, None),
        P("ra", "dec"),
        P("ra", "dec", None),
        P("ra", "dec", None),
        P("ra", "dec", None, None),
    )
    return jax.shard_map(
        on_device,
        mesh=mesh,
        in_specs=placed,
        out_specs=(P(("ra", "dec"), None, None), P(("ra", "dec"), None, None)),
        check_vma=False,
    )
```

```python
import functools
import math

import jax
import jax.numpy as jnp
from jax import lax
from jax.experimental import pallas as pl
from jax.experimental.pallas import tpu as pltpu
from jax.sharding import PartitionSpec as P

NBIN = 20
SAMPLES = 8
PATCH = 256
R_IN = 12
L_PATCH = 512
S_PATCH = 1024
REG_DEV = 8


growth_top = 23
growth_bottom = 20


def extended(block, sides, width, periodic):
    for axis, dim in sides:
        count = lax.axis_size(axis)
        forward = [(i, i + 1) for i in range(count - 1)]
        if periodic:
            forward.append((count - 1, 0))
        backward = [(target, source) for source, target in forward]
        low = lax.ppermute(
            lax.slice_in_dim(block, block.shape[dim] - width, None, axis=dim), axis, forward
        )
        high = lax.ppermute(lax.slice_in_dim(block, 0, width, axis=dim), axis, backward)
        block = jnp.concatenate([low, block, high], axis=dim)
    return block


def edge_squares():
    return [
        float((R_IN * growth_top**edge_level // growth_bottom**edge_level) ** 2)
        for edge_level in range(NBIN + 1)
    ]


def bin_scales():
    edge_sq = edge_squares()
    lens_per_cell = L_PATCH / (SAMPLES * REG_DEV)
    density = S_PATCH / (PATCH * PATCH)
    expected = [
        math.pi * (edge_sq[edge_level + 1] - edge_sq[edge_level]) * density * lens_per_cell
        for edge_level in range(NBIN)
    ]
    return jnp.array(expected, jnp.float32)


def ranks(keys):
    total = keys.shape[0]
    unique = keys * total + jnp.arange(total, dtype=jnp.int32)
    return jnp.sum((unique[None, :] < unique[:, None]).astype(jnp.int32), axis=1)


def compact_order(position_x, position_y, dead, strip_size):
    strip = ranks(position_x + 2 * PATCH * dead) // strip_size
    return ranks(strip * (4 * PATCH) + position_y + 2 * PATCH * dead)


def pair_kernel(edge_sq, groups, chunk, class_ref, lens_ref, place_ref, source_ref, catalog_ref, out_ref, crit, sums):
    patches, _, width = source_ref.shape
    tiles, _, tile = out_ref.shape
    pieces = width // chunk

    def crit_step(patch, carry):
        crit[patch] = lax.dot_general(
            source_ref[patch], lens_ref[...], (((0,), (0,)), ((), ())), preferred_element_type=jnp.float32
        )
        return carry

    lax.fori_loop(0, patches, crit_step, 0)

    def visit(first_edge, tile_index, patch, piece):
        columns = pl.ds(pl.multiple_of(tile_index * tile, tile), tile)
        rows = pl.ds(pl.multiple_of(piece * chunk, chunk), chunk)
        inverse_crit = crit[patch, rows, columns]
        catalog = catalog_ref[patch, rows, :]
        delta_x = catalog[:, 0:1] - place_ref[0:1, columns]
        delta_y = catalog[:, 1:2] - place_ref[1:2, columns]
        square_x = delta_x * delta_x
        square_y = delta_y * delta_y
        radius_sq = square_x + square_y
        inverse = 1.0 / jnp.maximum(radius_sq, edge_sq[0])
        turned = catalog[:, 2:3] * (square_x - square_y) + catalog[:, 3:4] * (delta_x * delta_y)
        signal = inverse_crit * (turned * inverse)
        weight = catalog[:, 4:5] * inverse_crit * inverse_crit
        for edge in range(first_edge, len(edge_sq)):
            inside = radius_sq < edge_sq[edge]
            for number, values in enumerate((signal, weight)):
                kept = jnp.where(inside, values, 0.0).reshape(chunk // 8, 8, tile)
                sums[edge, number] += jnp.sum(kept, axis=0)

    def tile_step(tile_index):
        sums[...] = jnp.zeros_like(sums)

        def chunk_step(index, inner):
            chosen = class_ref[tile_index, index]
            for number, first_edge in enumerate(groups):
                @pl.when(chosen == number)
                def _():
                    visit(first_edge, tile_index, index // pieces, index % pieces)
            return inner

        lax.fori_loop(0, patches * pieces, chunk_step, 0)
        totals = jnp.sum(sums[...], axis=2)
        out_ref[tile_index] = jnp.concatenate(
            [totals[1:, 0] - totals[:-1, 0], totals[1:, 1] - totals[:-1, 1]], axis=0
        )

    def guarded_step(tile_index, carry):
        @pl.when(class_ref[tile_index, patches * pieces] > 0)
        def _():
            tile_step(tile_index)

        @pl.when(class_ref[tile_index, patches * pieces] <= 0)
        def _():
            out_ref[tile_index] = jnp.zeros(out_ref.shape[1:], jnp.float32)

        return carry

    lax.fori_loop(0, tiles, guarded_step, 0)


def exchange_sum_kernel(table_ref, out_ref, first, partial, second, send_one, recv_one, send_two, recv_two):
    me_ra, me_dec = lax.axis_index("ra"), lax.axis_index("dec")
    count_ra, count_dec = lax.axis_size("ra"), lax.axis_size("dec")

    def peer_ra(step):
        return (lax.rem(me_ra + step, count_ra), me_dec)

    def peer_dec(step):
        return (me_ra, lax.rem(me_dec + step, count_dec))

    mesh_ids = pl.DeviceIdType.MESH
    barrier = pltpu.get_barrier_semaphore()
    for step in range(1, count_dec):
        pl.semaphore_signal(barrier, inc=1, device_id=peer_dec(step), device_id_type=mesh_ids)
    for step in range(1, count_ra):
        pl.semaphore_signal(barrier, inc=1, device_id=peer_ra(step), device_id_type=mesh_ids)
    pl.semaphore_wait(barrier, count_dec + count_ra - 2)

    copies = []
    for step in range(1, count_dec):
        copy = pltpu.make_async_remote_copy(
            src_ref=table_ref.at[lax.rem(me_dec + step, count_dec)],
            dst_ref=first.at[step - 1],
            send_sem=send_one.at[step - 1],
            recv_sem=recv_one.at[step - 1],
            device_id=peer_dec(step),
            device_id_type=mesh_ids,
        )
        copy.start()
        copies.append(copy)
    partial[...] = table_ref[me_dec]
    for step in range(1, count_dec):
        copies[step - 1].wait_recv()
        partial[...] += first[step - 1]
    late = []
    for step in range(1, count_ra):
        copy = pltpu.make_async_remote_copy(
            src_ref=partial.at[lax.rem(me_ra + step, count_ra)],
            dst_ref=second.at[step - 1],
            send_sem=send_two.at[step - 1],
            recv_sem=recv_two.at[step - 1],
            device_id=peer_ra(step),
            device_id_type=mesh_ids,
        )
        copy.start()
        late.append(copy)
    total = partial[me_ra]
    for step in range(1, count_ra):
        late[step - 1].wait_recv()
        total = total + second[step - 1]
    out_ref[...] = total
    for copy in copies + late:
        copy.wait_send()


def exchange_sum(table):
    count_dec, count_ra, rows, columns = table.shape
    return pl.pallas_call(
        exchange_sum_kernel,
        out_shape=jax.ShapeDtypeStruct((rows, columns), jnp.float32),
        in_specs=[pl.BlockSpec(memory_space=pltpu.VMEM)],
        out_specs=pl.BlockSpec(memory_space=pltpu.VMEM),
        scratch_shapes=[
            pltpu.VMEM((count_dec - 1, count_ra, rows, columns), jnp.float32),
            pltpu.VMEM((count_ra, rows, columns), jnp.float32),
            pltpu.VMEM((count_ra - 1, rows, columns), jnp.float32),
            pltpu.SemaphoreType.DMA((count_dec - 1,)),
            pltpu.SemaphoreType.DMA((count_dec - 1,)),
            pltpu.SemaphoreType.DMA((count_ra - 1,)),
            pltpu.SemaphoreType.DMA((count_ra - 1,)),
        ],
        compiler_params=pltpu.CompilerParams(
            collective_id=0, has_side_effects=True, vmem_limit_bytes=32 * 2**20
        ),
    )(table)


def on_device(lens_block, lens_count, lens_region, lens_sample, source_block):
    edge_sq = edge_squares()
    pdf_bins = source_block.shape[2] - 5
    width = source_block.shape[3]
    lens_total = lens_block.shape[3]
    tile = 128
    chunk = 64
    groups = (0, 8, 12, 14, 17, 18, 20)
    live_count = lens_count[0, 0]

    sources = source_block[0, 0]
    source_x = sources[pdf_bins].astype(jnp.int32)
    source_y = sources[pdf_bins + 1].astype(jnp.int32)
    source_rank = compact_order(source_x, source_y, jnp.zeros_like(source_x), width // 4)
    picked = (source_rank[:, None] == jnp.arange(width, dtype=jnp.int32)[None, :]).astype(jnp.bfloat16)
    sources = jnp.dot(sources, picked, preferred_element_type=jnp.float32).astype(jnp.bfloat16)
    partial_rows = extended(sources[None, None], (("ra", 0),), 1, True)
    beside_all = extended(partial_rows, (("dec", 1),), 1, False)
    beside_all = beside_all.reshape(9, sources.shape[0], width)

    lenses = lens_block[0, 0]
    slots = jnp.arange(lens_total, dtype=jnp.int32)
    dead = (slots >= live_count).astype(jnp.int32)
    lens_rank = compact_order(
        lenses[pdf_bins].astype(jnp.int32), lenses[pdf_bins + 1].astype(jnp.int32), dead, lens_total // 2
    )
    lens_hit = lens_rank[None, :] == slots[:, None]
    sorted_lenses = lax.dot_general(
        lenses, lens_hit.astype(jnp.bfloat16), (((1,), (1,)), ((), ())), preferred_element_type=jnp.float32
    )
    owner = lens_region[0, 0] // REG_DEV
    count_dec = lax.axis_size("dec")
    owner = owner % count_dec * lax.axis_size("ra") + owner // count_dec
    segment = (owner * REG_DEV + lens_region[0, 0] % REG_DEV) * SAMPLES + lens_sample[0, 0]
    segment = jnp.sum(jnp.where(lens_hit, segment[None, :], 0), axis=1)
    lens_kernel = sorted_lenses[:pdf_bins].astype(jnp.bfloat16)
    lens_places = sorted_lenses[pdf_bins:]
    lens_x, lens_y = lens_places[0], lens_places[1]

    catalog = beside_all[:, pdf_bins:].astype(jnp.float32)
    shift = jnp.arange(9, dtype=jnp.int32)
    shift_x = ((shift // 3 - 1) * PATCH).astype(jnp.float32)[:, None]
    shift_y = ((shift % 3 - 1) * PATCH).astype(jnp.float32)[:, None]
    placed_x = catalog[:, 0] + shift_x
    placed_y = catalog[:, 1] + shift_y
    source_weight = catalog[:, 4]
    zero_row = jnp.zeros_like(placed_x)
    rows = jnp.stack(
        [
            placed_x,
            placed_y,
            -source_weight * catalog[:, 2],
            -2.0 * source_weight * catalog[:, 3],
            source_weight,
            zero_row,
            zero_row,
            zero_row,
        ],
        axis=2,
    )

    def gap(lens_at, source_at):
        lens_at = lens_at.reshape(-1, 1, tile)
        source_at = source_at.reshape(1, -1, chunk)
        apart = jnp.maximum(
            source_at.min(axis=2) - lens_at.max(axis=2), lens_at.min(axis=2) - source_at.max(axis=2)
        )
        return jnp.maximum(apart, 0.0)

    gap_x = gap(lens_x, placed_x)
    gap_y = gap(lens_y, placed_y)
    nearest_sq = gap_x * gap_x + gap_y * gap_y
    classes = sum((nearest_sq >= edge_sq[first - 1]).astype(jnp.int32) for first in groups[1:])
    classes = classes + (nearest_sq >= edge_sq[-1]).astype(jnp.int32)
    live_tile = (jnp.arange(lens_total // tile, dtype=jnp.int32) * tile < live_count).astype(jnp.int32)
    classes = jnp.concatenate([classes, live_tile[:, None]], axis=1)

    totals = pl.pallas_call(
        functools.partial(pair_kernel, edge_sq, groups, chunk),
        out_shape=jax.ShapeDtypeStruct((lens_total // tile, 2 * NBIN, tile), jnp.float32),
        in_specs=[pl.BlockSpec(memory_space=pltpu.SMEM)] + [pl.BlockSpec(memory_space=pltpu.VMEM)] * 4,
        out_specs=pl.BlockSpec(memory_space=pltpu.VMEM),
        scratch_shapes=[
            pltpu.VMEM((9, width, lens_total), jnp.float32),
            pltpu.VMEM((NBIN + 1, 2, 8, tile), jnp.float32),
        ],
        compiler_params=pltpu.CompilerParams(vmem_limit_bytes=48 * 2**20),
    )(
        classes,
        lens_kernel,
        lens_places,
        beside_all[:, :pdf_bins],
        rows,
    )
    per_lens = jnp.transpose(totals, (0, 2, 1)).reshape(lens_total, 2 * NBIN)
    per_lens = jnp.where((slots < live_count)[:, None], per_lens, 0.0)
    count_ra, count_dec = lax.axis_size("ra"), lax.axis_size("dec")
    region_table = jax.ops.segment_sum(per_lens, segment, num_segments=REG_DEV * count_ra * count_dec * SAMPLES)
    region_table = region_table.reshape(count_dec, count_ra, REG_DEV * SAMPLES * 2 * NBIN // 128, 128)
    owned_rows = exchange_sum(region_table).reshape(-1, SAMPLES, 2, NBIN)
    scales = bin_scales()
    return (owned_rows[:, :, 0, :] / jnp.sqrt(scales), owned_rows[:, :, 1, :] / scales)


def solution(mesh):
    placed = (
        P("ra", "dec", None, None),
        P("ra", "dec"),
        P("ra", "dec", None),
        P("ra", "dec", None),
        P("ra", "dec", None, None),
    )
    return jax.shard_map(
        on_device,
        mesh=mesh,
        in_specs=placed,
        out_specs=(P(("ra", "dec"), None, None), P(("ra", "dec"), None, None)),
        check_vma=False,
    )
```

```python
import functools
import math

import jax
import jax.numpy as jnp
from jax import lax
from jax.experimental import pallas as pl
from jax.experimental.pallas import tpu as pltpu
from jax.sharding import PartitionSpec as P

NBIN = 20
SAMPLES = 8
PATCH = 256
R_IN = 12
L_PATCH = 512
S_PATCH = 1024
REG_DEV = 8


growth_top = 23
growth_bottom = 20


def extended(block, sides, width, periodic):
    for axis, dim in sides:
        count = lax.axis_size(axis)
        forward = [(i, i + 1) for i in range(count - 1)]
        if periodic:
            forward.append((count - 1, 0))
        backward = [(target, source) for source, target in forward]
        low = lax.ppermute(
            lax.slice_in_dim(block, block.shape[dim] - width, None, axis=dim), axis, forward
        )
        high = lax.ppermute(lax.slice_in_dim(block, 0, width, axis=dim), axis, backward)
        block = jnp.concatenate([low, block, high], axis=dim)
    return block


def edge_squares():
    return [
        float((R_IN * growth_top**edge_level // growth_bottom**edge_level) ** 2)
        for edge_level in range(NBIN + 1)
    ]


def bin_scales():
    edge_sq = edge_squares()
    lens_per_cell = L_PATCH / (SAMPLES * REG_DEV)
    density = S_PATCH / (PATCH * PATCH)
    expected = [
        math.pi * (edge_sq[edge_level + 1] - edge_sq[edge_level]) * density * lens_per_cell
        for edge_level in range(NBIN)
    ]
    return jnp.array(expected, jnp.float32)


def ranks(keys):
    total = keys.shape[0]
    unique = keys * total + jnp.arange(total, dtype=jnp.int32)
    return jnp.sum((unique[None, :] < unique[:, None]).astype(jnp.int32), axis=1)


def compact_order(position_x, position_y, dead, strip_size):
    strip = ranks(position_x + 2 * PATCH * dead) // strip_size
    return ranks(strip * (4 * PATCH) + position_y + 2 * PATCH * dead)


def pair_kernel(edge_sq, groups, chunk, tile, order_ref, start_ref, lens_ref, x_ref, y_ref, source_ref, catalog_ref, out_ref, crit, sums):
    patches, _, width = source_ref.shape
    tiles = out_ref.shape[0]
    pieces = width // chunk

    def crit_step(patch, carry):
        crit[patch] = jnp.dot(lens_ref[...], source_ref[patch], preferred_element_type=jnp.float32)
        return carry

    lax.fori_loop(0, patches, crit_step, 0)

    def visit(first_edge, tile_index, patch, piece):
        rows = pl.ds(pl.multiple_of(tile_index * tile, tile), tile)
        lens_x = x_ref[rows, :]
        lens_y = y_ref[rows, :]
        parts = []
        for part in range(chunk // 128):
            columns = pl.ds(pl.multiple_of(piece * chunk + part * 128, 128), 128)
            inverse_crit = crit[patch, rows, columns]
            catalog = catalog_ref[patch, :, columns]
            delta_x = catalog[0:1] - lens_x
            delta_y = catalog[1:2] - lens_y
            square_x = delta_x * delta_x
            square_y = delta_y * delta_y
            radius_sq = square_x + square_y
            inverse = 1.0 / jnp.maximum(radius_sq, edge_sq[0])
            turned = catalog[2:3] * (square_x - square_y) + catalog[3:4] * (delta_x * delta_y)
            signal = inverse_crit * (turned * inverse)
            weight = catalog[4:5] * inverse_crit * inverse_crit
            parts.append((radius_sq, signal, weight))
        for edge in range(first_edge, len(edge_sq)):
            masks = [radius_sq < edge_sq[edge] for radius_sq, _, _ in parts]
            signal_sum = sum(jnp.where(m, part[1], 0.0) for m, part in zip(masks, parts))
            weight_sum = sum(jnp.where(m, part[2], 0.0) for m, part in zip(masks, parts))
            sums[edge, 0] += signal_sum
            sums[edge, 1] += weight_sum

    ones = jnp.ones((8, 128), jnp.float32)

    def tile_step(tile_index, carry):
        sums[...] = jnp.zeros_like(sums)
        for number, first_edge in enumerate(groups):
            def chunk_step(place, inner, first_edge=first_edge):
                index = order_ref[tile_index, place]
                visit(first_edge, tile_index, index // pieces, index % pieces)
                return inner

            lax.fori_loop(start_ref[tile_index, number], start_ref[tile_index, number + 1], chunk_step, 0)
        out_ref[tile_index] = lax.dot_general(
            ones,
            sums[...].reshape(-1, 128),
            (((1,), (1,)), ((), ())),
            precision=lax.Precision.HIGHEST,
            preferred_element_type=jnp.float32,
        )
        return carry

    lax.fori_loop(0, tiles, tile_step, 0)


def exchange_sum_kernel(table_ref, out_ref, first, partial, second, send_one, recv_one, send_two, recv_two):
    me_ra, me_dec = lax.axis_index("ra"), lax.axis_index("dec")
    count_ra, count_dec = lax.axis_size("ra"), lax.axis_size("dec")

    def peer_ra(step):
        return (lax.rem(me_ra + step, count_ra), me_dec)

    def peer_dec(step):
        return (me_ra, lax.rem(me_dec + step, count_dec))

    mesh_ids = pl.DeviceIdType.MESH
    barrier = pltpu.get_barrier_semaphore()
    for step in range(1, count_dec):
        pl.semaphore_signal(barrier, inc=1, device_id=peer_dec(step), device_id_type=mesh_ids)
    for step in range(1, count_ra):
        pl.semaphore_signal(barrier, inc=1, device_id=peer_ra(step), device_id_type=mesh_ids)
    pl.semaphore_wait(barrier, count_dec + count_ra - 2)

    copies = []
    for step in range(1, count_dec):
        copy = pltpu.make_async_remote_copy(
            src_ref=table_ref.at[lax.rem(me_dec + step, count_dec)],
            dst_ref=first.at[step - 1],
            send_sem=send_one.at[step - 1],
            recv_sem=recv_one.at[step - 1],
            device_id=peer_dec(step),
            device_id_type=mesh_ids,
        )
        copy.start()
        copies.append(copy)
    partial[...] = table_ref[me_dec]
    for step in range(1, count_dec):
        copies[step - 1].wait_recv()
        partial[...] += first[step - 1]
    late = []
    for step in range(1, count_ra):
        copy = pltpu.make_async_remote_copy(
            src_ref=partial.at[lax.rem(me_ra + step, count_ra)],
            dst_ref=second.at[step - 1],
            send_sem=send_two.at[step - 1],
            recv_sem=recv_two.at[step - 1],
            device_id=peer_ra(step),
            device_id_type=mesh_ids,
        )
        copy.start()
        late.append(copy)
    total = partial[me_ra]
    for step in range(1, count_ra):
        late[step - 1].wait_recv()
        total = total + second[step - 1]
    out_ref[...] = total
    for copy in copies + late:
        copy.wait_send()


def exchange_sum(table):
    count_dec, count_ra, rows, columns = table.shape
    return pl.pallas_call(
        exchange_sum_kernel,
        out_shape=jax.ShapeDtypeStruct((rows, columns), jnp.float32),
        in_specs=[pl.BlockSpec(memory_space=pltpu.VMEM)],
        out_specs=pl.BlockSpec(memory_space=pltpu.VMEM),
        scratch_shapes=[
            pltpu.VMEM((count_dec - 1, count_ra, rows, columns), jnp.float32),
            pltpu.VMEM((count_ra, rows, columns), jnp.float32),
            pltpu.VMEM((count_ra - 1, rows, columns), jnp.float32),
            pltpu.SemaphoreType.DMA((count_dec - 1,)),
            pltpu.SemaphoreType.DMA((count_dec - 1,)),
            pltpu.SemaphoreType.DMA((count_ra - 1,)),
            pltpu.SemaphoreType.DMA((count_ra - 1,)),
        ],
        compiler_params=pltpu.CompilerParams(
            collective_id=0, has_side_effects=True, vmem_limit_bytes=32 * 2**20
        ),
    )(table)


def on_device(lens_block, lens_count, lens_region, lens_sample, source_block):
    edge_sq = edge_squares()
    pdf_bins = source_block.shape[2] - 5
    width = source_block.shape[3]
    lens_total = lens_block.shape[3]
    tile = 32
    chunk = 256
    groups = (0, 8, 12, 14, 17, 18, 20)
    live_count = lens_count[0, 0]

    sources = source_block[0, 0]
    source_x = sources[pdf_bins].astype(jnp.int32)
    source_y = sources[pdf_bins + 1].astype(jnp.int32)
    source_rank = compact_order(source_x, source_y, jnp.zeros_like(source_x), width // 2)
    picked = (source_rank[:, None] == jnp.arange(width, dtype=jnp.int32)[None, :]).astype(jnp.bfloat16)
    sources = jnp.dot(sources, picked, preferred_element_type=jnp.float32).astype(jnp.bfloat16)
    partial_rows = extended(sources[None, None], (("ra", 0),), 1, True)
    beside_all = extended(partial_rows, (("dec", 1),), 1, False)
    beside_all = beside_all.reshape(9, sources.shape[0], width)

    lenses = lens_block[0, 0]
    slots = jnp.arange(lens_total, dtype=jnp.int32)
    dead = (slots >= live_count).astype(jnp.int32)
    lens_rank = compact_order(
        lenses[pdf_bins].astype(jnp.int32), lenses[pdf_bins + 1].astype(jnp.int32), dead, lens_total // 4
    )
    lens_hit = lens_rank[None, :] == slots[:, None]
    sorted_lenses = lax.dot_general(
        lens_hit.astype(jnp.bfloat16), lenses, (((1,), (1,)), ((), ())), preferred_element_type=jnp.float32
    )
    owner = lens_region[0, 0] // REG_DEV
    count_dec = lax.axis_size("dec")
    owner = owner % count_dec * lax.axis_size("ra") + owner // count_dec
    segment = (owner * REG_DEV + lens_region[0, 0] % REG_DEV) * SAMPLES + lens_sample[0, 0]
    segment = jnp.sum(jnp.where(lens_hit, segment[None, :], 0), axis=1)
    lens_kernel = sorted_lenses[:, :pdf_bins].astype(jnp.bfloat16)
    lens_x = sorted_lenses[:, pdf_bins]
    lens_y = sorted_lenses[:, pdf_bins + 1]

    catalog = beside_all[:, pdf_bins:].astype(jnp.float32)
    shift = jnp.arange(9, dtype=jnp.int32)
    shift_x = ((shift // 3 - 1) * PATCH).astype(jnp.float32)[:, None]
    shift_y = ((shift % 3 - 1) * PATCH).astype(jnp.float32)[:, None]
    placed_x = catalog[:, 0] + shift_x
    placed_y = catalog[:, 1] + shift_y
    source_weight = catalog[:, 4]
    zero_row = jnp.zeros_like(placed_x)
    rows = jnp.stack(
        [
            placed_x,
            placed_y,
            -source_weight * catalog[:, 2],
            -2.0 * source_weight * catalog[:, 3],
            source_weight,
            zero_row,
            zero_row,
            zero_row,
        ],
        axis=1,
    )

    def gap(lens_at, source_at):
        lens_at = lens_at.reshape(-1, 1, tile)
        source_at = source_at.reshape(1, -1, chunk)
        apart = jnp.maximum(
            source_at.min(axis=2) - lens_at.max(axis=2), lens_at.min(axis=2) - source_at.max(axis=2)
        )
        return jnp.maximum(apart, 0.0)

    gap_x = gap(lens_x, placed_x)
    gap_y = gap(lens_y, placed_y)
    nearest_sq = gap_x * gap_x + gap_y * gap_y
    classes = sum((nearest_sq >= edge_sq[first - 1]).astype(jnp.int32) for first in groups[1:])
    classes = classes + (nearest_sq >= edge_sq[-1]).astype(jnp.int32)
    live_tile = jnp.arange(lens_total // tile, dtype=jnp.int32) * tile < live_count
    classes = jnp.where(live_tile[:, None], classes, len(groups))
    chunks = classes.shape[1]
    chunk_ids = jnp.arange(chunks, dtype=jnp.int32)
    unique = classes * chunks + chunk_ids[None, :]
    place = jnp.sum((unique[:, None, :] < unique[:, :, None]).astype(jnp.int32), axis=2)
    order = jnp.sum(jnp.where(place[:, None, :] == chunk_ids[None, :, None], chunk_ids[None, None, :], 0), axis=2)
    levels = jnp.arange(len(groups) + 1, dtype=jnp.int32)
    starts = jnp.sum((classes[:, None, :] < levels[None, :, None]).astype(jnp.int32), axis=2)

    totals = pl.pallas_call(
        functools.partial(pair_kernel, edge_sq, groups, chunk, tile),
        out_shape=jax.ShapeDtypeStruct((lens_total // tile, 8, 2 * (NBIN + 1) * tile), jnp.float32),
        in_specs=[pl.BlockSpec(memory_space=pltpu.SMEM)] * 2 + [pl.BlockSpec(memory_space=pltpu.VMEM)] * 5,
        out_specs=pl.BlockSpec(memory_space=pltpu.VMEM),
        scratch_shapes=[
            pltpu.VMEM((9, lens_total, width), jnp.float32),
            pltpu.VMEM((NBIN + 1, 2, tile, 128), jnp.float32),
        ],
        compiler_params=pltpu.CompilerParams(vmem_limit_bytes=48 * 2**20),
    )(
        order,
        starts,
        lens_kernel,
        jnp.broadcast_to(lens_x[:, None], (lens_total, 128)),
        jnp.broadcast_to(lens_y[:, None], (lens_total, 128)),
        beside_all[:, :pdf_bins],
        rows,
    )
    below = totals[:, 0].reshape(-1, NBIN + 1, 2, tile)
    per_bin = below[:, 1:] - below[:, :-1]
    per_lens = jnp.transpose(per_bin, (0, 3, 2, 1)).reshape(lens_total, 2 * NBIN)
    per_lens = jnp.where((slots < live_count)[:, None], per_lens, 0.0)
    count_ra, count_dec = lax.axis_size("ra"), lax.axis_size("dec")
    region_table = jax.ops.segment_sum(per_lens, segment, num_segments=REG_DEV * count_ra * count_dec * SAMPLES)
    region_table = region_table.reshape(count_dec, count_ra, REG_DEV * SAMPLES * 2 * NBIN // 128, 128)
    owned_rows = exchange_sum(region_table).reshape(-1, SAMPLES, 2, NBIN)
    scales = bin_scales()
    return (owned_rows[:, :, 0, :] / jnp.sqrt(scales), owned_rows[:, :, 1, :] / scales)


def solution(mesh):
    placed = (
        P("ra", "dec", None, None),
        P("ra", "dec"),
        P("ra", "dec", None),
        P("ra", "dec", None),
        P("ra", "dec", None, None),
    )
    return jax.shard_map(
        on_device,
        mesh=mesh,
        in_specs=placed,
        out_specs=(P(("ra", "dec"), None, None), P(("ra", "dec"), None, None)),
        check_vma=False,
    )
```

```python
import functools
import math

import jax
import jax.numpy as jnp
from jax import lax
from jax.experimental import pallas as pl
from jax.experimental.pallas import tpu as pltpu
from jax.sharding import PartitionSpec as P

NBIN = 20
SAMPLES = 8
PATCH = 256
R_IN = 12
L_PATCH = 512
S_PATCH = 1024
REG_DEV = 8


growth_top = 23
growth_bottom = 20


def extended(block, sides, width, periodic):
    for axis, dim in sides:
        count = lax.axis_size(axis)
        forward = [(i, i + 1) for i in range(count - 1)]
        if periodic:
            forward.append((count - 1, 0))
        backward = [(target, source) for source, target in forward]
        low = lax.ppermute(
            lax.slice_in_dim(block, block.shape[dim] - width, None, axis=dim), axis, forward
        )
        high = lax.ppermute(lax.slice_in_dim(block, 0, width, axis=dim), axis, backward)
        block = jnp.concatenate([low, block, high], axis=dim)
    return block


def edge_squares():
    return [
        float((R_IN * growth_top**edge_level // growth_bottom**edge_level) ** 2)
        for edge_level in range(NBIN + 1)
    ]


def bin_scales():
    edge_sq = edge_squares()
    lens_per_cell = L_PATCH / (SAMPLES * REG_DEV)
    density = S_PATCH / (PATCH * PATCH)
    expected = [
        math.pi * (edge_sq[edge_level + 1] - edge_sq[edge_level]) * density * lens_per_cell
        for edge_level in range(NBIN)
    ]
    return jnp.array(expected, jnp.float32)


def ranks(keys):
    total = keys.shape[0]
    unique = keys * total + jnp.arange(total, dtype=jnp.int32)
    return jnp.sum((unique[None, :] < unique[:, None]).astype(jnp.int32), axis=1)


def compact_order(position_x, position_y, dead, strip_size):
    strip = ranks(position_x + 2 * PATCH * dead) // strip_size
    return ranks(strip * (4 * PATCH) + position_y + 2 * PATCH * dead)


def pair_kernel(edge_sq, groups, chunk, tile, order_ref, start_ref, lens_ref, x_ref, y_ref, source_ref, catalog_ref, out_ref, crit, sums):
    patches, _, width = source_ref.shape
    pieces = width // chunk

    def crit_step(patch, carry):
        crit[patch] = jnp.dot(lens_ref[...], source_ref[patch], preferred_element_type=jnp.float32)
        return carry

    lax.fori_loop(0, patches, crit_step, 0)

    def visit(first_edge, tile_index, patch, piece):
        rows = pl.ds(pl.multiple_of(tile_index * tile, tile), tile)
        lens_x = x_ref[rows, :]
        lens_y = y_ref[rows, :]
        parts = []
        for part in range(chunk // 128):
            columns = pl.ds(pl.multiple_of(piece * chunk + part * 128, 128), 128)
            inverse_crit = crit[patch, rows, columns]
            catalog = catalog_ref[patch, :, columns]
            delta_x = catalog[0:1] - lens_x
            delta_y = catalog[1:2] - lens_y
            square_x = delta_x * delta_x
            square_y = delta_y * delta_y
            radius_sq = square_x + square_y
            inverse = 1.0 / jnp.maximum(radius_sq, edge_sq[0])
            turned = catalog[2:3] * (square_x - square_y) + catalog[3:4] * (delta_x * delta_y)
            signal = inverse_crit * (turned * inverse)
            weight = catalog[4:5] * inverse_crit * inverse_crit
            parts.append((radius_sq, signal, weight))
        for edge in range(first_edge, len(edge_sq)):
            masks = [radius_sq < edge_sq[edge] for radius_sq, _, _ in parts]
            signal_sum = sum(jnp.where(m, part[1], 0.0) for m, part in zip(masks, parts))
            weight_sum = sum(jnp.where(m, part[2], 0.0) for m, part in zip(masks, parts))
            sums[edge, 0] += signal_sum
            sums[edge, 1] += weight_sum

    ones = jnp.ones((8, 256), jnp.bfloat16)

    def tile_step(tile_index, carry):
        sums[...] = jnp.zeros_like(sums)
        for number, first_edge in enumerate(groups):
            def chunk_step(place, inner, first_edge=first_edge):
                index = order_ref[tile_index, place]
                visit(first_edge, tile_index, index // pieces, index % pieces)
                return inner

            lax.fori_loop(start_ref[tile_index, number], start_ref[tile_index, number + 1], chunk_step, 0)
        per_bin = (sums[1:] - sums[:-1]).reshape(-1, 128)
        high = per_bin.astype(jnp.bfloat16)
        low = (per_bin - high.astype(jnp.float32)).astype(jnp.bfloat16)
        out_ref[tile_index] = lax.dot_general(
            ones,
            jnp.concatenate([high, low], axis=1),
            (((1,), (1,)), ((), ())),
            preferred_element_type=jnp.float32,
        )
        return carry

    lax.fori_loop(0, start_ref[0, len(groups) + 1], tile_step, 0)


def exchange_sum_kernel(table_ref, out_ref, first, partial, second, send_one, recv_one, send_two, recv_two):
    me_ra, me_dec = lax.axis_index("ra"), lax.axis_index("dec")
    count_ra, count_dec = lax.axis_size("ra"), lax.axis_size("dec")

    def peer_ra(step):
        return (lax.rem(me_ra + step, count_ra), me_dec)

    def peer_dec(step):
        return (me_ra, lax.rem(me_dec + step, count_dec))

    mesh_ids = pl.DeviceIdType.MESH
    barrier = pltpu.get_barrier_semaphore()
    for step in range(1, count_dec):
        pl.semaphore_signal(barrier, inc=1, device_id=peer_dec(step), device_id_type=mesh_ids)
    for step in range(1, count_ra):
        pl.semaphore_signal(barrier, inc=1, device_id=peer_ra(step), device_id_type=mesh_ids)
    pl.semaphore_wait(barrier, count_dec + count_ra - 2)

    copies = []
    for step in range(1, count_dec):
        copy = pltpu.make_async_remote_copy(
            src_ref=table_ref.at[lax.rem(me_dec + step, count_dec)],
            dst_ref=first.at[step - 1],
            send_sem=send_one.at[step - 1],
            recv_sem=recv_one.at[step - 1],
            device_id=peer_dec(step),
            device_id_type=mesh_ids,
        )
        copy.start()
        copies.append(copy)
    partial[...] = table_ref[me_dec]
    for step in range(1, count_dec):
        copies[step - 1].wait_recv()
        partial[...] += first[step - 1]
    late = []
    for step in range(1, count_ra):
        copy = pltpu.make_async_remote_copy(
            src_ref=partial.at[lax.rem(me_ra + step, count_ra)],
            dst_ref=second.at[step - 1],
            send_sem=send_two.at[step - 1],
            recv_sem=recv_two.at[step - 1],
            device_id=peer_ra(step),
            device_id_type=mesh_ids,
        )
        copy.start()
        late.append(copy)
    total = partial[me_ra]
    for step in range(1, count_ra):
        late[step - 1].wait_recv()
        total = total + second[step - 1]
    out_ref[...] = total
    for copy in copies + late:
        copy.wait_send()


def exchange_sum(table):
    count_dec, count_ra, rows, columns = table.shape
    return pl.pallas_call(
        exchange_sum_kernel,
        out_shape=jax.ShapeDtypeStruct((rows, columns), jnp.float32),
        in_specs=[pl.BlockSpec(memory_space=pltpu.VMEM)],
        out_specs=pl.BlockSpec(memory_space=pltpu.VMEM),
        scratch_shapes=[
            pltpu.VMEM((count_dec - 1, count_ra, rows, columns), jnp.float32),
            pltpu.VMEM((count_ra, rows, columns), jnp.float32),
            pltpu.VMEM((count_ra - 1, rows, columns), jnp.float32),
            pltpu.SemaphoreType.DMA((count_dec - 1,)),
            pltpu.SemaphoreType.DMA((count_dec - 1,)),
            pltpu.SemaphoreType.DMA((count_ra - 1,)),
            pltpu.SemaphoreType.DMA((count_ra - 1,)),
        ],
        compiler_params=pltpu.CompilerParams(
            collective_id=0, has_side_effects=True, vmem_limit_bytes=32 * 2**20
        ),
    )(table)


def on_device(lens_block, lens_count, lens_region, lens_sample, source_block):
    edge_sq = edge_squares()
    pdf_bins = source_block.shape[2] - 5
    width = source_block.shape[3]
    lens_total = lens_block.shape[3]
    tile = 32
    chunk = 256
    groups = (0, 8, 12, 14, 17, 18, 20)
    live_count = lens_count[0, 0]

    sources = source_block[0, 0]
    source_x = sources[pdf_bins].astype(jnp.int32)
    source_y = sources[pdf_bins + 1].astype(jnp.int32)
    source_rank = compact_order(source_x, source_y, jnp.zeros_like(source_x), width // 2)
    picked = (source_rank[:, None] == jnp.arange(width, dtype=jnp.int32)[None, :]).astype(jnp.bfloat16)
    sources = jnp.dot(sources, picked, preferred_element_type=jnp.float32).astype(jnp.bfloat16)
    partial_rows = extended(sources[None, None], (("ra", 0),), 1, True)
    beside_all = extended(partial_rows, (("dec", 1),), 1, False)
    beside_all = beside_all.reshape(9, sources.shape[0], width)

    lenses = lens_block[0, 0]
    slots = jnp.arange(lens_total, dtype=jnp.int32)
    dead = (slots >= live_count).astype(jnp.int32)
    lens_rank = compact_order(
        lenses[pdf_bins].astype(jnp.int32), lenses[pdf_bins + 1].astype(jnp.int32), dead, lens_total // 4
    )
    lens_hit = lens_rank[None, :] == slots[:, None]
    sorted_lenses = lax.dot_general(
        lens_hit.astype(jnp.bfloat16), lenses, (((1,), (1,)), ((), ())), preferred_element_type=jnp.float32
    )
    owner = lens_region[0, 0] // REG_DEV
    count_dec = lax.axis_size("dec")
    owner = owner % count_dec * lax.axis_size("ra") + owner // count_dec
    segment = (owner * REG_DEV + lens_region[0, 0] % REG_DEV) * SAMPLES + lens_sample[0, 0]
    segment = jnp.sum(jnp.where(lens_hit, segment[None, :], 0), axis=1)
    lens_kernel = sorted_lenses[:, :pdf_bins].astype(jnp.bfloat16)
    lens_x = sorted_lenses[:, pdf_bins]
    lens_y = sorted_lenses[:, pdf_bins + 1]

    catalog = beside_all[:, pdf_bins:].astype(jnp.float32)
    shift = jnp.arange(9, dtype=jnp.int32)
    shift_x = ((shift // 3 - 1) * PATCH).astype(jnp.float32)[:, None]
    shift_y = ((shift % 3 - 1) * PATCH).astype(jnp.float32)[:, None]
    placed_x = catalog[:, 0] + shift_x
    placed_y = catalog[:, 1] + shift_y
    source_weight = catalog[:, 4]
    zero_row = jnp.zeros_like(placed_x)
    rows = jnp.stack(
        [
            placed_x,
            placed_y,
            -source_weight * catalog[:, 2],
            -2.0 * source_weight * catalog[:, 3],
            source_weight,
            zero_row,
            zero_row,
            zero_row,
        ],
        axis=1,
    )

    def gap(lens_at, source_at):
        lens_at = lens_at.reshape(-1, 1, tile)
        source_at = source_at.reshape(1, -1, chunk)
        apart = jnp.maximum(
            source_at.min(axis=2) - lens_at.max(axis=2), lens_at.min(axis=2) - source_at.max(axis=2)
        )
        return jnp.maximum(apart, 0.0)

    gap_x = gap(lens_x, placed_x)
    gap_y = gap(lens_y, placed_y)
    nearest_sq = gap_x * gap_x + gap_y * gap_y
    classes = sum((nearest_sq >= edge_sq[first - 1]).astype(jnp.int32) for first in groups[1:])
    classes = classes + (nearest_sq >= edge_sq[-1]).astype(jnp.int32)
    live_tile = jnp.arange(lens_total // tile, dtype=jnp.int32) * tile < live_count
    classes = jnp.where(live_tile[:, None], classes, len(groups))
    chunks = classes.shape[1]
    chunk_ids = jnp.arange(chunks, dtype=jnp.int32)
    unique = classes * chunks + chunk_ids[None, :]
    place = jnp.sum((unique[:, None, :] < unique[:, :, None]).astype(jnp.int32), axis=2)
    order = jnp.sum(jnp.where(place[:, None, :] == chunk_ids[None, :, None], chunk_ids[None, None, :], 0), axis=2)
    levels = jnp.arange(len(groups) + 1, dtype=jnp.int32)
    starts = jnp.sum((classes[:, None, :] < levels[None, :, None]).astype(jnp.int32), axis=2)
    live_tiles = jnp.broadcast_to(jnp.sum(live_tile.astype(jnp.int32)), (lens_total // tile, 1))
    starts = jnp.concatenate([starts, live_tiles], axis=1)

    totals = pl.pallas_call(
        functools.partial(pair_kernel, edge_sq, groups, chunk, tile),
        out_shape=jax.ShapeDtypeStruct((lens_total // tile, 8, 2 * NBIN * tile), jnp.float32),
        in_specs=[pl.BlockSpec(memory_space=pltpu.SMEM)] * 2 + [pl.BlockSpec(memory_space=pltpu.VMEM)] * 5,
        out_specs=pl.BlockSpec(memory_space=pltpu.VMEM),
        scratch_shapes=[
            pltpu.VMEM((9, lens_total, width), jnp.float32),
            pltpu.VMEM((NBIN + 1, 2, tile, 128), jnp.float32),
        ],
        compiler_params=pltpu.CompilerParams(vmem_limit_bytes=48 * 2**20),
    )(
        order,
        starts,
        lens_kernel,
        jnp.broadcast_to(lens_x[:, None], (lens_total, 128)),
        jnp.broadcast_to(lens_y[:, None], (lens_total, 128)),
        beside_all[:, :pdf_bins],
        rows,
    )
    per_bin = totals[:, 0].reshape(-1, NBIN, 2, tile)
    per_lens = jnp.transpose(per_bin, (0, 3, 2, 1)).reshape(lens_total, 2 * NBIN)
    per_lens = jnp.where((slots < live_count)[:, None], per_lens, 0.0)
    count_ra, count_dec = lax.axis_size("ra"), lax.axis_size("dec")
    region_table = jax.ops.segment_sum(per_lens, segment, num_segments=REG_DEV * count_ra * count_dec * SAMPLES)
    region_table = region_table.reshape(count_dec, count_ra, REG_DEV * SAMPLES * 2 * NBIN // 128, 128)
    owned_rows = exchange_sum(region_table).reshape(-1, SAMPLES, 2, NBIN)
    scales = bin_scales()
    return (owned_rows[:, :, 0, :] / jnp.sqrt(scales), owned_rows[:, :, 1, :] / scales)


def solution(mesh):
    placed = (
        P("ra", "dec", None, None),
        P("ra", "dec"),
        P("ra", "dec", None),
        P("ra", "dec", None),
        P("ra", "dec", None, None),
    )
    return jax.shard_map(
        on_device,
        mesh=mesh,
        in_specs=placed,
        out_specs=(P(("ra", "dec"), None, None), P(("ra", "dec"), None, None)),
        check_vma=False,
    )
```

```python
import functools
import math

import jax
import jax.numpy as jnp
from jax import lax
from jax.experimental import pallas as pl
from jax.experimental.pallas import tpu as pltpu
from jax.sharding import PartitionSpec as P

NBIN = 20
SAMPLES = 8
PATCH = 256
R_IN = 12
L_PATCH = 512
S_PATCH = 1024
REG_DEV = 8


growth_top = 23
growth_bottom = 20


def extended(block, sides, width, periodic):
    for axis, dim in sides:
        count = lax.axis_size(axis)
        forward = [(i, i + 1) for i in range(count - 1)]
        if periodic:
            forward.append((count - 1, 0))
        backward = [(target, source) for source, target in forward]
        low = lax.ppermute(
            lax.slice_in_dim(block, block.shape[dim] - width, None, axis=dim), axis, forward
        )
        high = lax.ppermute(lax.slice_in_dim(block, 0, width, axis=dim), axis, backward)
        block = jnp.concatenate([low, block, high], axis=dim)
    return block


def edge_squares():
    return [
        float((R_IN * growth_top**edge_level // growth_bottom**edge_level) ** 2)
        for edge_level in range(NBIN + 1)
    ]


def bin_scales():
    edge_sq = edge_squares()
    lens_per_cell = L_PATCH / (SAMPLES * REG_DEV)
    density = S_PATCH / (PATCH * PATCH)
    expected = [
        math.pi * (edge_sq[edge_level + 1] - edge_sq[edge_level]) * density * lens_per_cell
        for edge_level in range(NBIN)
    ]
    return jnp.array(expected, jnp.float32)


def ranks(keys):
    total = keys.shape[0]
    unique = keys * total + jnp.arange(total, dtype=jnp.int32)
    return jnp.sum((unique[None, :] < unique[:, None]).astype(jnp.int32), axis=1)


def compact_order(position_x, position_y, dead, strip_size):
    strip = ranks(position_x + 2 * PATCH * dead) // strip_size
    return ranks(strip * (4 * PATCH) + position_y + 2 * PATCH * dead)


def pair_kernel(edge_sq, groups, chunk, tile, order_ref, start_ref, lens_ref, x_ref, y_ref, source_ref, catalog_ref, out_ref, crit, sums):
    patches, _, width = source_ref.shape
    pieces = width // chunk

    def crit_step(patch, carry):
        crit[patch] = jnp.dot(lens_ref[...], source_ref[patch], preferred_element_type=jnp.float32)
        return carry

    lax.fori_loop(0, patches, crit_step, 0)

    def visit(first_edge, tile_index, patch, piece):
        rows = pl.ds(pl.multiple_of(tile_index * tile, tile), tile)
        lens_x = x_ref[rows, :]
        lens_y = y_ref[rows, :]
        parts = []
        for part in range(chunk // 128):
            columns = pl.ds(pl.multiple_of(piece * chunk + part * 128, 128), 128)
            inverse_crit = crit[patch, rows, columns]
            catalog = catalog_ref[patch, :, columns]
            delta_x = catalog[0:1] - lens_x
            delta_y = catalog[1:2] - lens_y
            square_x = delta_x * delta_x
            square_y = delta_y * delta_y
            radius_sq = square_x + square_y
            inverse = 1.0 / jnp.maximum(radius_sq, edge_sq[0])
            turned = catalog[2:3] * (square_x - square_y) + catalog[3:4] * (delta_x * delta_y)
            signal = inverse_crit * (turned * inverse)
            weight = catalog[4:5] * inverse_crit * inverse_crit
            parts.append((radius_sq, signal, weight))
        for edge in range(first_edge, len(edge_sq)):
            masks = [radius_sq < edge_sq[edge] for radius_sq, _, _ in parts]
            signal_sum = sum(jnp.where(m, part[1], 0.0) for m, part in zip(masks, parts))
            weight_sum = sum(jnp.where(m, part[2], 0.0) for m, part in zip(masks, parts))
            sums[edge, 0] += signal_sum
            sums[edge, 1] += weight_sum

    ones = jnp.ones((8, 256), jnp.bfloat16)

    def tile_step(tile_index, carry):
        sums[...] = jnp.zeros_like(sums)
        for number, first_edge in enumerate(groups):
            def chunk_step(place, inner, first_edge=first_edge):
                index = order_ref[tile_index, place]
                visit(first_edge, tile_index, index // pieces, index % pieces)
                return inner

            lax.fori_loop(start_ref[tile_index, number], start_ref[tile_index, number + 1], chunk_step, 0)
        per_bin = (sums[1:] - sums[:-1]).reshape(-1, 128)
        high = per_bin.astype(jnp.bfloat16)
        low = (per_bin - high.astype(jnp.float32)).astype(jnp.bfloat16)
        out_ref[tile_index] = lax.dot_general(
            ones,
            jnp.concatenate([high, low], axis=1),
            (((1,), (1,)), ((), ())),
            preferred_element_type=jnp.float32,
        )
        return carry

    lax.fori_loop(0, start_ref[0, len(groups) + 1], tile_step, 0)


def exchange_sum_kernel(table_ref, out_ref, first, partial, second, send_one, recv_one, send_two, recv_two):
    me_ra, me_dec = lax.axis_index("ra"), lax.axis_index("dec")
    count_ra, count_dec = lax.axis_size("ra"), lax.axis_size("dec")

    def peer_ra(step):
        return (lax.rem(me_ra + step, count_ra), me_dec)

    def peer_dec(step):
        return (me_ra, lax.rem(me_dec + step, count_dec))

    mesh_ids = pl.DeviceIdType.MESH
    barrier = pltpu.get_barrier_semaphore()
    for step in range(1, count_dec):
        pl.semaphore_signal(barrier, inc=1, device_id=peer_dec(step), device_id_type=mesh_ids)
    for step in range(1, count_ra):
        pl.semaphore_signal(barrier, inc=1, device_id=peer_ra(step), device_id_type=mesh_ids)
    pl.semaphore_wait(barrier, count_dec + count_ra - 2)

    copies = []
    for step in range(1, count_dec):
        copy = pltpu.make_async_remote_copy(
            src_ref=table_ref.at[lax.rem(me_dec + step, count_dec)],
            dst_ref=first.at[step - 1],
            send_sem=send_one.at[step - 1],
            recv_sem=recv_one.at[step - 1],
            device_id=peer_dec(step),
            device_id_type=mesh_ids,
        )
        copy.start()
        copies.append(copy)
    partial[...] = table_ref[me_dec]
    for step in range(1, count_dec):
        copies[step - 1].wait_recv()
        partial[...] += first[step - 1]
    late = []
    for step in range(1, count_ra):
        copy = pltpu.make_async_remote_copy(
            src_ref=partial.at[lax.rem(me_ra + step, count_ra)],
            dst_ref=second.at[step - 1],
            send_sem=send_two.at[step - 1],
            recv_sem=recv_two.at[step - 1],
            device_id=peer_ra(step),
            device_id_type=mesh_ids,
        )
        copy.start()
        late.append(copy)
    total = partial[me_ra]
    for step in range(1, count_ra):
        late[step - 1].wait_recv()
        total = total + second[step - 1]
    out_ref[...] = total
    for copy in copies + late:
        copy.wait_send()


def exchange_sum(table):
    count_dec, count_ra, rows, columns = table.shape
    return pl.pallas_call(
        exchange_sum_kernel,
        out_shape=jax.ShapeDtypeStruct((rows, columns), jnp.float32),
        in_specs=[pl.BlockSpec(memory_space=pltpu.VMEM)],
        out_specs=pl.BlockSpec(memory_space=pltpu.VMEM),
        scratch_shapes=[
            pltpu.VMEM((count_dec - 1, count_ra, rows, columns), jnp.float32),
            pltpu.VMEM((count_ra, rows, columns), jnp.float32),
            pltpu.VMEM((count_ra - 1, rows, columns), jnp.float32),
            pltpu.SemaphoreType.DMA((count_dec - 1,)),
            pltpu.SemaphoreType.DMA((count_dec - 1,)),
            pltpu.SemaphoreType.DMA((count_ra - 1,)),
            pltpu.SemaphoreType.DMA((count_ra - 1,)),
        ],
        compiler_params=pltpu.CompilerParams(
            collective_id=0, has_side_effects=True, vmem_limit_bytes=32 * 2**20
        ),
    )(table)


def on_device(lens_block, lens_count, lens_region, lens_sample, source_block):
    edge_sq = edge_squares()
    pdf_bins = source_block.shape[2] - 5
    width = source_block.shape[3]
    lens_total = lens_block.shape[3]
    tile = 32
    chunk = 128
    groups = (0, 8, 12, 14, 17, 18, 20)
    live_count = lens_count[0, 0]

    sources = source_block[0, 0]
    source_x = sources[pdf_bins].astype(jnp.int32)
    source_y = sources[pdf_bins + 1].astype(jnp.int32)
    source_rank = compact_order(source_x, source_y, jnp.zeros_like(source_x), width // 4)
    picked = (source_rank[:, None] == jnp.arange(width, dtype=jnp.int32)[None, :]).astype(jnp.bfloat16)
    sources = jnp.dot(sources, picked, preferred_element_type=jnp.float32).astype(jnp.bfloat16)
    partial_rows = extended(sources[None, None], (("ra", 0),), 1, True)
    beside_all = extended(partial_rows, (("dec", 1),), 1, False)
    beside_all = beside_all.reshape(9, sources.shape[0], width)

    lenses = lens_block[0, 0]
    slots = jnp.arange(lens_total, dtype=jnp.int32)
    dead = (slots >= live_count).astype(jnp.int32)
    lens_rank = compact_order(
        lenses[pdf_bins].astype(jnp.int32), lenses[pdf_bins + 1].astype(jnp.int32), dead, lens_total // 4
    )
    lens_hit = lens_rank[None, :] == slots[:, None]
    sorted_lenses = lax.dot_general(
        lens_hit.astype(jnp.bfloat16), lenses, (((1,), (1,)), ((), ())), preferred_element_type=jnp.float32
    )
    owner = lens_region[0, 0] // REG_DEV
    count_dec = lax.axis_size("dec")
    owner = owner % count_dec * lax.axis_size("ra") + owner // count_dec
    segment = (owner * REG_DEV + lens_region[0, 0] % REG_DEV) * SAMPLES + lens_sample[0, 0]
    segment = jnp.sum(jnp.where(lens_hit, segment[None, :], 0), axis=1)
    lens_kernel = sorted_lenses[:, :pdf_bins].astype(jnp.bfloat16)
    lens_x = sorted_lenses[:, pdf_bins]
    lens_y = sorted_lenses[:, pdf_bins + 1]

    catalog = beside_all[:, pdf_bins:].astype(jnp.float32)
    shift = jnp.arange(9, dtype=jnp.int32)
    shift_x = ((shift // 3 - 1) * PATCH).astype(jnp.float32)[:, None]
    shift_y = ((shift % 3 - 1) * PATCH).astype(jnp.float32)[:, None]
    placed_x = catalog[:, 0] + shift_x
    placed_y = catalog[:, 1] + shift_y
    source_weight = catalog[:, 4]
    zero_row = jnp.zeros_like(placed_x)
    rows = jnp.stack(
        [
            placed_x,
            placed_y,
            -source_weight * catalog[:, 2],
            -2.0 * source_weight * catalog[:, 3],
            source_weight,
            zero_row,
            zero_row,
            zero_row,
        ],
        axis=1,
    )

    def gap(lens_at, source_at):
        lens_at = lens_at.reshape(-1, 1, tile)
        source_at = source_at.reshape(1, -1, chunk)
        apart = jnp.maximum(
            source_at.min(axis=2) - lens_at.max(axis=2), lens_at.min(axis=2) - source_at.max(axis=2)
        )
        return jnp.maximum(apart, 0.0)

    gap_x = gap(lens_x, placed_x)
    gap_y = gap(lens_y, placed_y)
    nearest_sq = gap_x * gap_x + gap_y * gap_y
    classes = sum((nearest_sq >= edge_sq[first - 1]).astype(jnp.int32) for first in groups[1:])
    classes = classes + (nearest_sq >= edge_sq[-1]).astype(jnp.int32)
    live_tile = jnp.arange(lens_total // tile, dtype=jnp.int32) * tile < live_count
    classes = jnp.where(live_tile[:, None], classes, len(groups))
    chunks = classes.shape[1]
    chunk_ids = jnp.arange(chunks, dtype=jnp.int32)
    unique = classes * chunks + chunk_ids[None, :]
    place = jnp.sum((unique[:, None, :] < unique[:, :, None]).astype(jnp.int32), axis=2)
    order = jnp.sum(jnp.where(place[:, None, :] == chunk_ids[None, :, None], chunk_ids[None, None, :], 0), axis=2)
    levels = jnp.arange(len(groups) + 1, dtype=jnp.int32)
    starts = jnp.sum((classes[:, None, :] < levels[None, :, None]).astype(jnp.int32), axis=2)
    live_tiles = jnp.broadcast_to(jnp.sum(live_tile.astype(jnp.int32)), (lens_total // tile, 1))
    starts = jnp.concatenate([starts, live_tiles], axis=1)

    totals = pl.pallas_call(
        functools.partial(pair_kernel, edge_sq, groups, chunk, tile),
        out_shape=jax.ShapeDtypeStruct((lens_total // tile, 8, 2 * NBIN * tile), jnp.float32),
        in_specs=[pl.BlockSpec(memory_space=pltpu.SMEM)] * 2 + [pl.BlockSpec(memory_space=pltpu.VMEM)] * 5,
        out_specs=pl.BlockSpec(memory_space=pltpu.VMEM),
        scratch_shapes=[
            pltpu.VMEM((9, lens_total, width), jnp.float32),
            pltpu.VMEM((NBIN + 1, 2, tile, 128), jnp.float32),
        ],
        compiler_params=pltpu.CompilerParams(vmem_limit_bytes=48 * 2**20),
    )(
        order,
        starts,
        lens_kernel,
        jnp.broadcast_to(lens_x[:, None], (lens_total, 128)),
        jnp.broadcast_to(lens_y[:, None], (lens_total, 128)),
        beside_all[:, :pdf_bins],
        rows,
    )
    per_bin = totals[:, 0].reshape(-1, NBIN, 2, tile)
    per_lens = jnp.transpose(per_bin, (0, 3, 2, 1)).reshape(lens_total, 2 * NBIN)
    per_lens = jnp.where((slots < live_count)[:, None], per_lens, 0.0)
    count_ra, count_dec = lax.axis_size("ra"), lax.axis_size("dec")
    region_table = jax.ops.segment_sum(per_lens, segment, num_segments=REG_DEV * count_ra * count_dec * SAMPLES)
    region_table = region_table.reshape(count_dec, count_ra, REG_DEV * SAMPLES * 2 * NBIN // 128, 128)
    owned_rows = exchange_sum(region_table).reshape(-1, SAMPLES, 2, NBIN)
    scales = bin_scales()
    return (owned_rows[:, :, 0, :] / jnp.sqrt(scales), owned_rows[:, :, 1, :] / scales)


def solution(mesh):
    placed = (
        P("ra", "dec", None, None),
        P("ra", "dec"),
        P("ra", "dec", None),
        P("ra", "dec", None),
        P("ra", "dec", None, None),
    )
    return jax.shard_map(
        on_device,
        mesh=mesh,
        in_specs=placed,
        out_specs=(P(("ra", "dec"), None, None), P(("ra", "dec"), None, None)),
        check_vma=False,
    )
```
